32 devices in a mesh: section: 2 (over y), ctx: 4 (over z), dp: 4 (over x, core).
Axes of the slice: x: 2, y: 2, z: 4, core: 2. Of those that a mesh axis runs over, the one named last changes fastest.
Arguments:
- activations: bfloat16 [2, 4, 512, 1280], P('section', 'dp', 'ctx'), may hold values from -6 to 6
- out_grads: bfloat16 [2, 4, 512, 1280], P('section', 'dp', 'ctx'), may hold values from -6 to 6
- doc_ids: int32 [4, 4], replicated, may hold values from 0 to 1, never falling along the last dimension, each value on 1 to 3 neighbouring positions
- query_weight: bfloat16 [2, 1280, 640], P('section', None, 'dp'), may hold values from -0.195655948 to 0.195655948
- key_weight: bfloat16 [2, 1280, 640], P('section', None, 'dp'), may hold values from -3.0745935 to 3.0745935
- value_weight: bfloat16 [2, 1280, 640], P('section', None, 'dp'), may hold values from -0.15625 to 0.15625
- out_weight: bfloat16 [2, 640, 1280], P('section', 'dp'), may hold values from -0.25 to 0.25
Outputs:
- received_grad: bfloat16 [2, 4, 512, 1280], P('section', 'dp', 'ctx')
The draws below stay inside these ranges and needn't reach their ends.
Inputs may be any that keep to these rules, and one draw needn't show every extreme that they name: `doc_ids`: each page stack's documents are runs of whole blocks, numbered from 0 in order; a document covers at most 3 blocks.
All inputs are finite; a program needn't handle non-finite values.
Results may differ from the reference program's by a relative error of at most 0.0085.
The reference program's roundings to bfloat16 on the way count: a program that leaves them out, or rounds other values in their place, can miss the bound.
Values may be sent and summed in bfloat16 or wider, within the bound.
No kernel may reach another device: no remote copies, remote signals or barrier semaphores. Data moves between devices by JAX's collectives and lax.ppermute only.
A program may use at most 128 MiB of HBM per device.

```python
import math
import jax
import jax.numpy as jnp
import numpy as np
from jax import lax

D = 1280
HEADS = 8
HEAD_DIM = 80
BLOCK = 128
LENGTH = 512
NB = 4
PAGES = 4
N_SECTION = 2


def weight_base(key):
    raw = jax.random.normal(jax.random.fold_in(key, 11), (N_SECTION, D, HEADS * HEAD_DIM), jnp.float32)
    return jnp.clip(raw, -4.0, 4.0) * (1.7 * D ** (-0.5))


def draw_query_weight(key, part):
    return weight_base(key).astype(jnp.bfloat16)


def draw_key_weight(key, part):
    raw = jax.random.normal(jax.random.fold_in(key, 12), (N_SECTION, D, HEADS * HEAD_DIM), jnp.float32)
    result = jnp.clip(raw, -4.0, 4.0) * D ** (-0.5)
    return result.astype(jnp.bfloat16)


def draw_activations(key, part):
    shape = (N_SECTION, PAGES, LENGTH, D)
    result = jnp.clip(jax.random.normal(jax.random.fold_in(key, 23), shape, jnp.float32), -6.0, 6.0)
    return result.astype(jnp.bfloat16)


def steps_of(key, dims, cuts, least, high):
    loudness = 1.0
    for dim, blocks in cuts:
        steps = jax.random.uniform(jax.random.fold_in(jax.random.fold_in(key, 6), dim), (blocks,), jnp.float32, least / len(cuts), high / len(cuts))
        loudness = loudness * jnp.repeat(jnp.exp(steps), dims[dim] // blocks).reshape((-1,) + (1,) * (len(dims) - 1 - dim))
    return loudness


def length_profile(amount, total, reach, lean):
    portions = [(1 << 20) // math.isqrt(standing ** lean) + 1 for standing in range(2, amount + 1)]
    rest, holding = total - reach - (amount - 1), [1] * (amount - 1)
    while rest > 0:
        movable = [i for i in range(amount - 1) if holding[i] < reach]
        mass, budget = sum([portions[i] for i in movable]), rest
        for i in movable:
            addition = min(reach - holding[i], max(1, budget * portions[i] // mass), rest)
            holding[i] = holding[i] + addition
            rest = rest - addition
    return np.array([reach] + holding)


def uneven_parts(rng, count, total, bound, slope):
    if count == 2:
        one = jax.random.randint(rng, (), max(1, total - bound), min(bound, total - 1) + 1)
        return jnp.stack([one, total - one])
    lengths = jnp.asarray(length_profile(count, total, bound, slope), jnp.int32)
    couples = (count - 1) // 2
    source_of, receiver = lengths[1:1 + 2 * couples:2], lengths[2:2 + 2 * couples:2]
    margin = jnp.minimum(source_of - 1, bound - receiver)
    shifted = jax.random.randint(jax.random.fold_in(rng, 1), (couples,), 0, 1 << 20) % (margin + 1)
    lengths = lengths.at[1:1 + 2 * couples:2].set(source_of - shifted).at[2:2 + 2 * couples:2].set(receiver + shifted)
    return lengths[jax.random.permutation(jax.random.fold_in(rng, 2), count)]


def scatter_about(rng, shape, spread, reach, shards=(), dtype=jnp.bfloat16):
    drawn = spread * jax.random.normal(rng, shape, jnp.float32)
    if shards:
        drawn = drawn * steps_of(rng, shape, shards, -0.22, 0.18)
    return jnp.clip(drawn, -reach, reach).astype(dtype)


def setup_inputs(seed: int = 0) -> dict:
    seeds = jax.random.split(jax.random.key(seed), 8)
    return {
        "activations": draw_activations(jax.random.fold_in(seeds[7], 71), 0),
        "out_grads": scatter_about(seeds[1], (N_SECTION, PAGES, LENGTH, D), 1.0, 6.0, ((0, 2), (1, 4), (2, 4))),
        "doc_ids": jax.vmap(lambda own: jnp.searchsorted(jnp.cumsum(uneven_parts(own, max(2, NB // 4), NB, 3 * NB // 4, 2)), jnp.arange(NB), side="right"))(jax.random.split(seeds[2], PAGES)).reshape((PAGES, NB)).astype(jnp.int32),
        "query_weight": draw_query_weight(jax.random.fold_in(seeds[7], 71), 0),
        "key_weight": draw_key_weight(jax.random.fold_in(seeds[7], 71), 0),
        "value_weight": scatter_about(seeds[5], (N_SECTION, D, HEADS * HEAD_DIM), D ** -0.5, 0.15625, ((0, 2), (2, 4))),
        "out_weight": scatter_about(seeds[6], (N_SECTION, HEADS * HEAD_DIM, D), (HEADS * HEAD_DIM) ** -0.5, 0.25, ((0, 2), (1, 4))),
    }


NEG = -1e+30

def layer_grad(inputs_low, upstream, page_ids, query_proj, key_proj, value_proj, out_proj):
    length = inputs_low.shape[0]
    score_scale = HEAD_DIM ** (-0.5)
    highest = lax.Precision.HIGHEST
    inputs = inputs_low.astype(jnp.float32)
    inv_rms = lax.rsqrt(lax.optimization_barrier(jnp.mean(inputs * inputs, axis=-1, keepdims=True)) + 1e-05)
    normed = (inputs * inv_rms).astype(jnp.bfloat16)
    queries = jnp.dot(normed, query_proj, preferred_element_type=jnp.float32)
    key_rows = jnp.dot(normed, key_proj, preferred_element_type=jnp.float32)
    values = jnp.dot(normed, value_proj, preferred_element_type=jnp.float32).astype(jnp.bfloat16)
    out_grad = jnp.dot(upstream, out_proj.T, preferred_element_type=jnp.float32).astype(jnp.bfloat16)
    block_doc = page_ids[(jnp.arange(length) // BLOCK).astype(jnp.int32)]
    allowed = block_doc[:, None] == block_doc[None, :]

    def split_heads(matrix):
        return matrix.reshape(length, HEADS, HEAD_DIM).transpose(1, 0, 2)

    def one_head(parts):
        head_q = parts[0].astype(jnp.float32)
        head_k = parts[1].astype(jnp.float32)
        head_v = parts[2].astype(jnp.float32)
        head_g = parts[3].astype(jnp.float32)
        scores = jnp.dot(head_q, head_k.T, precision=highest) * score_scale
        scores = jnp.where(allowed, scores, NEG)
        top_score = lax.optimization_barrier(jnp.max(scores, axis=-1, keepdims=True))
        total = lax.optimization_barrier(jnp.sum(jnp.where(allowed, jnp.exp(scores - top_score), 0.0), axis=-1, keepdims=True))
        log_total = top_score + jnp.log(total)
        prob = jnp.where(allowed, jnp.exp(scores - log_total), 0.0)
        dprob = jnp.dot(head_g, head_v.T, precision=highest)
        row_delta = lax.optimization_barrier(jnp.sum(prob * dprob, axis=-1, keepdims=True))
        dscore = prob * (dprob - row_delta)
        dscore_low = lax.optimization_barrier(dscore.astype(jnp.bfloat16)).astype(jnp.float32)
        prob_low = lax.optimization_barrier(prob.astype(jnp.bfloat16)).astype(jnp.float32)
        q_grad = (jnp.dot(dscore_low, head_k, precision=highest) * score_scale).astype(jnp.bfloat16)
        k_grad = (jnp.dot(dscore_low.T, head_q, precision=highest) * score_scale).astype(jnp.bfloat16)
        v_grad = jnp.dot(prob_low.T, head_g, precision=highest).astype(jnp.bfloat16)
        return (q_grad, k_grad, v_grad)
    head_grads = lax.map(one_head, (split_heads(queries), split_heads(key_rows), split_heads(values), split_heads(out_grad)))

    def merge_heads(stacked):
        return stacked.transpose(1, 0, 2).reshape(length, HEADS * HEAD_DIM)
    q_grad = merge_heads(head_grads[0])
    k_grad = merge_heads(head_grads[1])
    v_grad = merge_heads(head_grads[2])
    normed_grad = jnp.dot(q_grad, query_proj.T, preferred_element_type=jnp.float32)
    normed_grad = normed_grad + jnp.dot(k_grad, key_proj.T, preferred_element_type=jnp.float32)
    normed_grad = normed_grad + jnp.dot(v_grad, value_proj.T, preferred_element_type=jnp.float32)
    branch = inv_rms * normed_grad - inputs * inv_rms ** 3 * lax.optimization_barrier(jnp.mean(normed_grad * inputs, axis=-1, keepdims=True))
    return branch.astype(jnp.bfloat16)

def reference(activations, out_grads, doc_ids, query_weight, key_weight, value_weight, out_weight):

    def per_section(section_parts):
        section_inputs, section_upstream, section_q, section_k, section_v, section_o = section_parts

        def per_page(page_parts):
            return layer_grad(page_parts[0], page_parts[1], page_parts[2], section_q, section_k, section_v, section_o)
        return lax.map(per_page, (section_inputs, section_upstream, doc_ids))
    branches = lax.map(per_section, (activations, out_grads, query_weight, key_weight, value_weight, out_weight))
    return jnp.roll(branches, -1, axis=0)
```

```python
import functools
import math

import jax
import jax.numpy as jnp
from jax import lax
from jax.experimental import pallas as pl
from jax.experimental.pallas import tpu as pltpu
from jax.sharding import PartitionSpec as P

HEAD_DIM = 80
BLOCK = 128
QKV = 3 * HEAD_DIM
NEG = -1e30
SCALE = HEAD_DIM**-0.5
LOG2E = math.log2(math.e)
F32 = jnp.float32
BF16 = jnp.bfloat16


def dot_nn(a, b):
    return lax.dot_general(a, b, (((1,), (0,)), ((), ())), preferred_element_type=F32)


def dot_nt(a, b):
    return lax.dot_general(a, b, (((1,), (1,)), ((), ())), preferred_element_type=F32)


def split(x):
    high = x.astype(BF16)
    return high, (x - high.astype(F32)).astype(BF16)


def inverse_rms(x):
    return lax.rsqrt(jnp.mean(x * x, axis=-1, keepdims=True) + 1e-05)


def window_flags(ids_ref, count):
    page, me, blocks = lax.axis_index("dp"), lax.axis_index("ctx"), lax.axis_size("ctx")
    mine = ids_ref[page, me]

    def same(at):
        inside = jnp.clip(at, 0, blocks - 1)
        return (inside == at) & (ids_ref[page, inside] == mine)

    flags = []
    for place in range(1, count):
        behind = same(me - place)
        flags.append((behind, behind | same(me + count - place)))
    return flags


def masks(flags):
    ones = jnp.ones((1, BLOCK), F32)
    row_mask = jnp.concatenate([ones] + [ones * valid.astype(F32) for _, valid in flags], axis=1)
    window = row_mask.shape[1]
    first = lax.broadcasted_iota(jnp.int32, (16, window), 0) == 0
    key_bias = jnp.where(first, 1.0 - row_mask, 0.0).astype(BF16)
    query_bias = jnp.where(first, NEG, 0.0).astype(BF16)
    return key_bias, query_bias, row_mask


def heads_backward(packs, grads, normed, key_bias, query_bias, row_mask):
    window = normed.shape[1]
    chunk = min(window, 384)
    qkv = [dot_nn(pack, normed) for pack in packs]
    queries, keys = [], []
    key_rows, value_rows = [], []
    for part in qkv:
        q_high, q_low = split(part[:HEAD_DIM] * (SCALE * LOG2E))
        k_high, k_low = split(part[HEAD_DIM : 2 * HEAD_DIM])
        queries.append(jnp.concatenate([q_high, q_high, q_low, query_bias], axis=0))
        keys.append(jnp.concatenate([k_high, k_low], axis=0))
        key_rows.append(jnp.concatenate([k_high, k_low, k_high, key_bias], axis=0).T)
        value_rows.append(part[2 * HEAD_DIM :].astype(BF16).T)

    heads = range(len(packs))
    own_query, own_key, own_value = [None for _ in heads], [0.0 for _ in heads], [0.0 for _ in heads]
    for start in range(0, window, chunk):
        cols = slice(start, start + chunk)
        scores = [dot_nn(key_rows[h], queries[h][:, cols]) for h in heads]
        dprob = [dot_nn(value_rows[h], grads[h][:, cols]) for h in heads]
        weights, inverse, delta = [], [], []
        for h in heads:
            weights.append(jnp.exp2(scores[h] - jnp.max(scores[h], axis=0, keepdims=True)))
            total = 1.0 / jnp.sum(weights[h], axis=0, keepdims=True)
            delta.append(jnp.sum(weights[h] * dprob[h], axis=0, keepdims=True) * total)
            inverse.append(total * row_mask[:, cols])
        for h in heads:
            prob = weights[h][:BLOCK] * inverse[h]
            dscore = (prob * (dprob[h][:BLOCK] - delta[h])).astype(BF16)
            own_value[h] = own_value[h] + dot_nt(grads[h][:, cols], prob.astype(BF16))
            own_key[h] = own_key[h] + dot_nt(queries[h][HEAD_DIM:QKV, cols], dscore)
            if start == 0:
                dscore_rows = (
                    weights[h][:, :BLOCK]
                    * inverse[h][:, :BLOCK]
                    * (dprob[h][:, :BLOCK] - delta[h][:, :BLOCK])
                ).astype(BF16)
                own_query[h] = dot_nn(keys[h], dscore_rows)
    result = None
    for h in heads:
        q_grad = ((own_query[h][:HEAD_DIM] + own_query[h][HEAD_DIM:]) * SCALE).astype(BF16)
        k_grad = ((own_key[h][:HEAD_DIM] + own_key[h][HEAD_DIM:]) * (1.0 / LOG2E)).astype(BF16)
        rows = jnp.concatenate([q_grad, k_grad, own_value[h].astype(BF16)], axis=0).T
        part = dot_nn(rows, packs[h])
        result = part if result is None else result + part
    return result


def for_place(index, count, flags, fill):
    if index == 0:
        fill(0)
        return
    behind = flags[index - 1][0]
    even = lax.rem(lax.axis_index("ctx"), 2) == 0
    for is_behind, is_even in ((a, b) for a in (True, False) for b in (True, False)):
        distance = index if is_behind else count - index
        slot = 2 * distance - 1 if is_behind != is_even else 2 * distance

        @pl.when((behind == is_behind) & (even == is_even))
        def _():
            fill(slot)


def transposed_normed(input_ref):
    x = input_ref[...].astype(F32)
    return (x * inverse_rms(x)).astype(BF16).T


def pack_kernel(*refs):
    weights, (local_ref, shared_ref, sems) = refs[:3], refs[3:]
    even = lax.rem(lax.axis_index("ctx"), 2) == 0

    def to(ref, at):
        return ref.at[pl.ds(at * HEAD_DIM, HEAD_DIM), :]

    heads = local_ref.shape[0] // QKV
    copies = [
        pltpu.make_async_copy(
            to(weights[at], h), to(local_ref, 3 * h + at), sems.at[3 * h + at]
        )
        for h in range(heads)
        for at in range(3)
    ]
    for copy in copies:
        copy.start()
    for copy in copies:
        copy.wait()
    shared_ref[:HEAD_DIM, :] = local_ref[QKV + HEAD_DIM : QKV + 2 * HEAD_DIM, :]
    for is_even, at in ((True, 0), (False, 2)):

        @pl.when(even == is_even)
        def _():
            first = QKV + at * HEAD_DIM
            shared_ref[HEAD_DIM:, :] = local_ref[first : first + HEAD_DIM, :]


def start_kernel(input_ref, grad_ref, even_ref, odd_ref, *refs):
    *weight_refs, normed_ref, to_even_ref, to_odd_ref = refs
    width = normed_ref.shape[0]
    normed_ref[...] = transposed_normed(input_ref)
    to_even_ref[:width, :] = transposed_normed(odd_ref)
    to_odd_ref[:width, :] = transposed_normed(even_ref)
    grad_rows(grad_ref, weight_refs, (to_even_ref, to_odd_ref), width)


def grad_rows(grad_ref, weight_refs, rows_refs, start):
    for weight_ref in weight_refs:
        size = weight_ref.shape[0]
        part = dot_nt(weight_ref[...], grad_ref[...]).astype(BF16)
        for rows_ref in rows_refs:
            rows_ref[start : start + size, :] = part
        start += size


def relay_kernel(skip, grad_ref, even_ref, odd_ref, *refs):
    *weight_refs, to_even_ref, to_odd_ref = refs
    rows = even_ref.shape[0] - skip
    to_even_ref[:rows, :] = odd_ref[skip:, :]
    to_odd_ref[:rows, :] = even_ref[skip:, :]
    grad_rows(grad_ref, weight_refs, (to_even_ref, to_odd_ref), rows)


def first_kernel(count, grad_at, ids_ref, *refs):
    slots = 2 * count - 1
    blocks, grad_slots = refs[:slots], refs[slots : 2 * slots]
    *pack_refs, normed_ref, total_ref, window_ref = refs[2 * slots :]
    width, rows = normed_ref.shape[0], window_ref.shape[0]
    flags = window_flags(ids_ref, count)
    for index in range(count):

        def fill(slot):
            cols = pl.ds(index * BLOCK, BLOCK)
            normed_ref[:, cols] = blocks[slot][:width, :]
            window_ref[:, cols] = grad_slots[slot][grad_at[slot] : grad_at[slot] + rows, :]

        for_place(index, count, flags, fill)
    packs = [ref[at : at + QKV, :] for ref in pack_refs for at in range(0, ref.shape[0], QKV)]
    grads = [window_ref[h * HEAD_DIM : (h + 1) * HEAD_DIM, :] for h in range(len(packs))]
    total_ref[...] = heads_backward(packs, grads, normed_ref[...], *masks(flags))


def next_kernel(count, grad_at, places, shared, last, ids_ref, *refs):
    slots = 2 * count - 1
    grad_slots = refs[:slots]
    per_head = 2 if shared else 1
    normed_ref, so_far_ref, *pieces = refs[slots : slots + 2 + per_head * len(places)]
    *rest, total_ref, window_ref, pack_ref = refs[slots + 2 + per_head * len(places) :]
    flags = window_flags(ids_ref, count)
    for index in range(count):

        def fill(slot):
            cols = pl.ds(index * BLOCK, BLOCK)
            for at, h in enumerate(places):
                to = slice(at * HEAD_DIM, (at + 1) * HEAD_DIM)
                start = grad_at[slot] + h * HEAD_DIM
                window_ref[to, cols] = grad_slots[slot][start : start + HEAD_DIM, :]

        for_place(index, count, flags, fill)
    packs, grads = [], []
    even = lax.rem(lax.axis_index("ctx"), 2) == 0
    for at in range(len(places)):
        if shared:
            mine, other = pieces[2 * at : 2 * at + 2]
            pack_ref[at, HEAD_DIM : 2 * HEAD_DIM, :] = mine[:HEAD_DIM, :]
            for is_even in (True, False):

                @pl.when(even == is_even)
                def _():
                    low, high = mine[HEAD_DIM:, :], other[...]
                    pack_ref[at, :HEAD_DIM, :] = low if is_even else high
                    pack_ref[at, 2 * HEAD_DIM :, :] = high if is_even else low

            packs.append(pack_ref[at])
        else:
            packs.append(pieces[at][...])
        grads.append(window_ref[at * HEAD_DIM : (at + 1) * HEAD_DIM, :])
    total = so_far_ref[...] + heads_backward(packs, grads, normed_ref[...], *masks(flags))
    if last:
        x = rest[0][...].astype(F32)
        inv_rms = inverse_rms(x)
        branch = inv_rms * total - x * inv_rms**3 * jnp.mean(total * x, axis=-1, keepdims=True)
        total_ref[...] = branch.astype(BF16)
    else:
        total_ref[...] = total


def call(kernel, operands, out_shape, window, scratch=(), scalars=True, space=pltpu.VMEM):
    vmem = pl.BlockSpec(memory_space=pltpu.VMEM)
    specs = [pl.BlockSpec(memory_space=pltpu.SMEM)] if scalars else []
    if space != pltpu.VMEM:
        operands = [pltpu.with_memory_space_constraint(ref, space) for ref in operands]
    return pl.pallas_call(
        kernel,
        out_shape=out_shape,
        in_specs=specs + [pl.BlockSpec(memory_space=space)] * (len(operands) - len(specs)),
        out_specs=jax.tree.map(lambda _: vmem, out_shape),
        scratch_shapes=list(scratch),
        compiler_params=pltpu.CompilerParams(vmem_limit_bytes=(8 << 20) + window * (32 << 10)),
        cost_estimate=pl.CostEstimate(flops=1000, bytes_accessed=1000, transcendentals=0),
    )(*operands)


def pair_swap(array, first):
    length, width = lax.axis_size("ctx"), lax.axis_size("dp")
    pairs = []
    for i in range(length):
        low = i - (i - first) % 2
        for d in range(width):
            if low >= 0 and low + 1 < length:
                pairs.append((i * width + d, (2 * low + 1 - i) * width + d))
            else:
                pairs.append((i * width + d, i * width + (d ^ 1)))
    return lax.ppermute(array, ("ctx", "dp"), pairs)


def pair_steps(even, odd):
    return pair_swap(odd, 0), pair_swap(even, 1)


def after(values, *others):
    return lax.optimization_barrier((values, others))[0]


def dp_swap(array, by):
    return lax.ppermute(array, "dp", [(i, i ^ by) for i in range(lax.axis_size("dp"))])


def body(activations, out_grads, doc_ids, query_weight, key_weight, value_weight, out_weight):
    own_input, own_grad = activations[0, 0], out_grads[0, 0]
    width = own_input.shape[-1]
    count = 3 * lax.axis_size("ctx") // 4
    window = count * BLOCK
    heads = query_weight.shape[2] // HEAD_DIM

    sized = lambda rows, columns, dtype: jax.ShapeDtypeStruct((rows, columns), dtype)
    some = 2 * heads * HEAD_DIM

    own_out = out_weight[0]
    far_out = dp_swap(own_out, 2)
    near_out = dp_swap(own_out, 1)
    steps = [pair_steps(own_input, own_input)]
    local, shared = call(
        pack_kernel,
        [query_weight[0].T, key_weight[0].T, value_weight[0].T],
        (sized(heads * QKV, width, BF16), sized(2 * HEAD_DIM, width, BF16)),
        window,
        scratch=[pltpu.SemaphoreType.DMA((3 * heads,))],
        scalars=False,
        space=pltpu.HBM,
    )
    far_shared = dp_swap(shared, 2)
    near = dp_swap(after(local, steps[0], far_out, near_out), 1)

    normed, near_grad, to_odd_first = call(
        start_kernel,
        [own_input, own_grad, *steps[0], own_out, near_out],
        (sized(width, BLOCK, BF16),) + (sized(width + some, BLOCK, BF16),) * 2,
        window,
        scalars=False,
    )
    steps.append(pair_steps(to_odd_first, near_grad))
    far_near_out = dp_swap(far_out, 1)
    skip = width if count == 3 else 0
    far_grad, to_odd = call(
        functools.partial(relay_kernel, skip),
        [after(own_grad, near), *steps[1], far_out, far_near_out],
        (sized(steps[1][0].shape[0] - skip + some, BLOCK, BF16),) * 2,
        window,
        scalars=False,
    )
    steps.append(pair_steps(to_odd, far_grad))
    far_whole = dp_swap(after(local[:QKV], far_out, far_grad), 2)
    while len(steps) < count + 1:
        drop = {count - 1: width, count: some}.get(len(steps), 0)
        steps.append(pair_steps(*(ref[drop:] for ref in steps[-1])))

    def slots(own, first, until_end):
        pairs = [pair for pair in steps[first : first + count - 1]]
        refs = [own] + [ref for pair in pairs for ref in pair]
        return refs, [ref.shape[0] - until_end for ref in refs]

    first_pair = (to_odd_first, near_grad)
    normed_slots = [normed] + [ref for pair in [first_pair] + steps[1 : count - 1] for ref in pair]
    grad_slots, _ = slots(near_grad, 1, 0)
    grad_at = [ref.shape[0] - some for ref in grad_slots[:3]]
    grad_at += [ref.shape[0] - 2 * some for ref in grad_slots[3:]]
    window_normed, total = call(
        functools.partial(first_kernel, count, grad_at),
        [doc_ids, *normed_slots, *grad_slots, local, near],
        (sized(width, window, BF16), sized(BLOCK, width, F32)),
        window,
        scratch=[pltpu.VMEM((some, window), BF16)],
    )

    far_near_shared = dp_swap(after(far_shared, steps[2]), 1)
    ctx_edge = pair_swap(after(far_shared, steps[2])[HEAD_DIM:], 0)
    far_near_edge = dp_swap(after(ctx_edge, total), 1)
    grad_slots, grad_at = slots(far_grad, 2, some)

    def add(total, places, shared, pieces, extra=()):
        return call(
            functools.partial(next_kernel, count, grad_at, places, shared, bool(extra)),
            [doc_ids, *grad_slots, window_normed, total, *pieces, *extra],
            sized(BLOCK, width, BF16 if extra else F32),
            window,
            scratch=[
                pltpu.VMEM((len(places) * HEAD_DIM, window), BF16),
                pltpu.VMEM((len(places), QKV, width), BF16),
            ],
        )

    pieces = (far_shared, ctx_edge, far_near_shared, far_near_edge)
    total = add(total, (1, heads + 1), True, pieces)
    far_near_whole = dp_swap(after(far_whole, total), 1)
    total = add(total, (0,), False, [far_whole])
    result = add(total, (heads,), False, [far_near_whole], [own_input])
    sections = lax.axis_size("section")
    result = lax.ppermute(result, "section", [(i, (i - 1) % sections) for i in range(sections)])
    return result[None, None]


def solution(mesh):
    return jax.shard_map(
        body,
        mesh=mesh,
        in_specs=(
            P("section", "dp", "ctx", None),
            P("section", "dp", "ctx", None),
            P(),
            P("section", None, "dp"),
            P("section", None, "dp"),
            P("section", None, "dp"),
            P("section", "dp", None),
        ),
        out_specs=P("section", "dp", "ctx", None),
        check_vma=False,
    )
```

```python
import functools
import math

import jax
import jax.numpy as jnp
from jax import lax
from jax.experimental import pallas as pl
from jax.experimental.pallas import tpu as pltpu
from jax.sharding import PartitionSpec as P

HEAD_DIM = 80
BLOCK = 128
QKV = 3 * HEAD_DIM
NEAR_CUT = 320
NEG = -1e30
SCALE = HEAD_DIM**-0.5
LOG2E = math.log2(math.e)
F32 = jnp.float32
BF16 = jnp.bfloat16


def dot_nn(a, b):
    return lax.dot_general(a, b, (((1,), (0,)), ((), ())), preferred_element_type=F32)


def dot_nt(a, b):
    return lax.dot_general(a, b, (((1,), (1,)), ((), ())), preferred_element_type=F32)


def split(x):
    high = x.astype(BF16)
    return high, (x - high.astype(F32)).astype(BF16)


def inverse_rms(x):
    return lax.rsqrt(jnp.mean(x * x, axis=-1, keepdims=True) + 1e-05)


def window_flags(ids_ref, count):
    page, me, blocks = lax.axis_index("dp"), lax.axis_index("ctx"), lax.axis_size("ctx")
    mine = ids_ref[page, me]

    def same(at):
        inside = jnp.clip(at, 0, blocks - 1)
        return (inside == at) & (ids_ref[page, inside] == mine)

    flags = []
    for place in range(1, count):
        behind = same(me - place)
        flags.append((behind, behind | same(me + count - place)))
    return flags


def masks(flags):
    ones = jnp.ones((1, BLOCK), F32)
    row_mask = jnp.concatenate([ones] + [ones * valid.astype(F32) for _, valid in flags], axis=1)
    window = row_mask.shape[1]
    first = lax.broadcasted_iota(jnp.int32, (16, window), 0) == 0
    key_bias = jnp.where(first, 1.0 - row_mask, 0.0).astype(BF16)
    query_bias = jnp.where(first, NEG, 0.0).astype(BF16)
    return key_bias, query_bias, row_mask


def heads_backward(packs, grads, normed, key_bias, query_bias, row_mask):
    window = normed.shape[1]
    chunk = min(window, 384)
    qkv = [dot_nn(pack, normed) for pack in packs]
    queries, keys = [], []
    key_rows, value_rows = [], []
    for part in qkv:
        q_high, q_low = split(part[:HEAD_DIM] * (SCALE * LOG2E))
        k_high, k_low = split(part[HEAD_DIM : 2 * HEAD_DIM])
        queries.append(jnp.concatenate([q_high, q_high, q_low, query_bias], axis=0))
        keys.append(jnp.concatenate([k_high, k_low], axis=0))
        key_rows.append(jnp.concatenate([k_high, k_low, k_high, key_bias], axis=0).T)
        value_rows.append(part[2 * HEAD_DIM :].astype(BF16).T)

    heads = range(len(packs))
    own_query, own_key, own_value = [None for _ in heads], [0.0 for _ in heads], [0.0 for _ in heads]
    for start in range(0, window, chunk):
        cols = slice(start, start + chunk)
        scores = [dot_nn(key_rows[h], queries[h][:, cols]) for h in heads]
        dprob = [dot_nn(value_rows[h], grads[h][:, cols]) for h in heads]
        weights, inverse, delta = [], [], []
        for h in heads:
            weights.append(jnp.exp2(scores[h] - jnp.max(scores[h], axis=0, keepdims=True)))
            total = 1.0 / jnp.sum(weights[h], axis=0, keepdims=True)
            delta.append(jnp.sum(weights[h] * dprob[h], axis=0, keepdims=True) * total)
            inverse.append(total * row_mask[:, cols])
        for h in heads:
            prob = weights[h][:BLOCK] * inverse[h]
            dscore = (prob * (dprob[h][:BLOCK] - delta[h])).astype(BF16)
            own_value[h] = own_value[h] + dot_nt(grads[h][:, cols], prob.astype(BF16))
            own_key[h] = own_key[h] + dot_nt(queries[h][HEAD_DIM:QKV, cols], dscore)
            if start == 0:
                dscore_rows = (
                    weights[h][:, :BLOCK]
                    * inverse[h][:, :BLOCK]
                    * (dprob[h][:, :BLOCK] - delta[h][:, :BLOCK])
                ).astype(BF16)
                own_query[h] = dot_nn(keys[h], dscore_rows)
    result = None
    for h in heads:
        q_grad = ((own_query[h][:HEAD_DIM] + own_query[h][HEAD_DIM:]) * SCALE).astype(BF16)
        k_grad = ((own_key[h][:HEAD_DIM] + own_key[h][HEAD_DIM:]) * (1.0 / LOG2E)).astype(BF16)
        rows = jnp.concatenate([q_grad, k_grad, own_value[h].astype(BF16)], axis=0).T
        part = dot_nn(rows, packs[h])
        result = part if result is None else result + part
    return result


def for_place(index, count, flags, fill):
    if index == 0:
        fill(0)
        return
    behind = flags[index - 1][0]
    even = lax.rem(lax.axis_index("ctx"), 2) == 0
    for is_behind, is_even in ((a, b) for a in (True, False) for b in (True, False)):
        distance = index if is_behind else count - index
        slot = 2 * distance - 1 if is_behind != is_even else 2 * distance

        @pl.when((behind == is_behind) & (even == is_even))
        def _():
            fill(slot)


def transposed_normed(input_ref):
    x = input_ref[...].astype(F32)
    return (x * inverse_rms(x)).astype(BF16).T


def pack_kernel(*refs):
    *weights, local_ref, sems = refs
    heads = local_ref.shape[0] // QKV

    def part(ref, at):
        return ref.at[pl.ds(at * HEAD_DIM, HEAD_DIM), :]

    pairs = [(part(weights[at], h), part(local_ref, 3 * h + at)) for h in range(heads) for at in range(3)]
    copies = [pltpu.make_async_copy(*pair, sems.at[i]) for i, pair in enumerate(pairs)]
    for copy in copies:
        copy.start()
    for copy in copies:
        copy.wait()


def start_kernel(input_ref, grad_ref, even_ref, odd_ref, *refs):
    *weight_refs, normed_ref, to_even_ref, to_odd_ref = refs
    width = normed_ref.shape[0]
    normed_ref[...] = transposed_normed(input_ref)
    to_even_ref[:width, :] = transposed_normed(odd_ref)
    to_odd_ref[:width, :] = transposed_normed(even_ref)
    grad_rows(grad_ref, weight_refs, (to_even_ref, to_odd_ref), width)


def grad_rows(grad_ref, weight_refs, rows_refs, start):
    for weight_ref in weight_refs:
        size = weight_ref.shape[0]
        part = dot_nt(weight_ref[...], grad_ref[...]).astype(BF16)
        for rows_ref in rows_refs:
            rows_ref[start : start + size, :] = part
        start += size


def relay_kernel(skip, grad_ref, even_ref, odd_ref, *refs):
    *weight_refs, to_even_ref, to_odd_ref = refs
    rows = even_ref.shape[0] - skip
    to_even_ref[:rows, :] = odd_ref[skip:, :]
    to_odd_ref[:rows, :] = even_ref[skip:, :]
    grad_rows(grad_ref, weight_refs, (to_even_ref, to_odd_ref), rows)


def first_kernel(count, grad_at, ids_ref, *refs):
    slots = 2 * count - 1
    blocks, grad_slots = refs[:slots], refs[slots : 2 * slots]
    *pack_refs, normed_ref, total_ref, window_ref = refs[2 * slots :]
    width, rows = normed_ref.shape[0], window_ref.shape[0]
    flags = window_flags(ids_ref, count)
    for index in range(count):

        def fill(slot):
            cols = pl.ds(index * BLOCK, BLOCK)
            normed_ref[:, cols] = blocks[slot][:width, :]
            window_ref[:, cols] = grad_slots[slot][grad_at[slot] : grad_at[slot] + rows, :]

        for_place(index, count, flags, fill)
    local_ref, *near_refs = pack_refs
    near = jnp.concatenate([ref[...] for ref in near_refs], axis=0)
    starts = range(0, local_ref.shape[0], QKV)
    packs = [local_ref[at : at + QKV, :] for at in starts] + [near[at : at + QKV] for at in starts]
    grads = [window_ref[h * HEAD_DIM : (h + 1) * HEAD_DIM, :] for h in range(len(packs))]
    total_ref[...] = heads_backward(packs, grads, normed_ref[...], *masks(flags))


def next_kernel(count, grad_at, places, last, ids_ref, *refs):
    slots = 2 * count - 1
    grad_slots = refs[:slots]
    normed_ref, so_far_ref, *rest, total_ref, window_ref = refs[slots:]
    if last:
        *rest, input_ref = rest
    flags = window_flags(ids_ref, count)
    for index in range(count):

        def fill(slot):
            cols = pl.ds(index * BLOCK, BLOCK)
            for at, h in enumerate(places):
                to = slice(at * HEAD_DIM, (at + 1) * HEAD_DIM)
                start = grad_at[slot] + h * HEAD_DIM
                window_ref[to, cols] = grad_slots[slot][start : start + HEAD_DIM, :]

        for_place(index, count, flags, fill)
    packs = [rest[0][...]]
    if len(places) > 1:
        packs.append(jnp.concatenate([ref[...] for ref in rest[1:]], axis=0))
    grads = [window_ref[at * HEAD_DIM : (at + 1) * HEAD_DIM, :] for at in range(len(places))]
    total = so_far_ref[...] + heads_backward(packs, grads, normed_ref[...], *masks(flags))
    if last:
        x = input_ref[...].astype(F32)
        inv_rms = inverse_rms(x)
        branch = inv_rms * total - x * inv_rms**3 * jnp.mean(total * x, axis=-1, keepdims=True)
        total_ref[...] = branch.astype(BF16)
    else:
        total_ref[...] = total


def call(kernel, operands, out_shape, window, scratch=(), scalars=True, space=pltpu.VMEM):
    vmem = pl.BlockSpec(memory_space=pltpu.VMEM)
    specs = [pl.BlockSpec(memory_space=pltpu.SMEM)] if scalars else []
    if space != pltpu.VMEM:
        operands = [pltpu.with_memory_space_constraint(ref, space) for ref in operands]
    return pl.pallas_call(
        kernel,
        out_shape=out_shape,
        in_specs=specs + [pl.BlockSpec(memory_space=space)] * (len(operands) - len(specs)),
        out_specs=jax.tree.map(lambda _: vmem, out_shape),
        scratch_shapes=list(scratch),
        compiler_params=pltpu.CompilerParams(vmem_limit_bytes=(8 << 20) + window * (32 << 10)),
        cost_estimate=pl.CostEstimate(flops=1000, bytes_accessed=1000, transcendentals=0),
    )(*operands)


def pair_swap(array, first):
    length, width = lax.axis_size("ctx"), lax.axis_size("dp")
    pairs = []
    for i in range(length):
        low = i - (i - first) % 2
        for d in range(width):
            if low >= 0 and low + 1 < length:
                pairs.append((i * width + d, (2 * low + 1 - i) * width + d))
            else:
                pairs.append((i * width + d, i * width + (d ^ 1)))
    return lax.ppermute(array, ("ctx", "dp"), pairs)


def pair_steps(even, odd):
    return pair_swap(odd, 0), pair_swap(even, 1)


def after(values, *others):
    return lax.optimization_barrier((values, others))[0]


def dp_swap(array, by):
    return lax.ppermute(array, "dp", [(i, i ^ by) for i in range(lax.axis_size("dp"))])


def body(activations, out_grads, doc_ids, query_weight, key_weight, value_weight, out_weight):
    own_input, own_grad = activations[0, 0], out_grads[0, 0]
    width = own_input.shape[-1]
    count = 3 * lax.axis_size("ctx") // 4
    window = count * BLOCK
    heads = query_weight.shape[2] // HEAD_DIM

    sized = lambda rows, columns, dtype: jax.ShapeDtypeStruct((rows, columns), dtype)
    some = 2 * heads * HEAD_DIM

    out_rows = heads * HEAD_DIM
    own_out = out_weight[0]
    far_out = dp_swap(own_out, 2)
    near_out = dp_swap(own_out, 1)
    steps = [pair_steps(own_input, own_input)]
    local = call(
        pack_kernel,
        [query_weight[0].T, key_weight[0].T, value_weight[0].T],
        sized(heads * QKV, width, BF16),
        window,
        scratch=[pltpu.SemaphoreType.DMA((3 * heads,))],
        scalars=False,
        space=pltpu.HBM,
    )
    near = [dp_swap(part, 1) for part in (local[:NEAR_CUT], local[NEAR_CUT:])]
    far_last = dp_swap(local[QKV : 2 * QKV], 2)

    normed, near_grad, first_odd = call(
        start_kernel,
        [own_input, after(own_grad, far_out), *steps[0], own_out, near_out],
        (sized(width, BLOCK, BF16),) + (sized(width + some, BLOCK, BF16),) * 2,
        window,
        scalars=False,
    )
    steps.append(pair_steps(first_odd, near_grad))
    far_out = after(far_out, normed)
    far_near_out = [dp_swap(far_out[at : at + HEAD_DIM], 1) for at in range(0, out_rows, HEAD_DIM)]
    skip = width if count == 3 else 0
    far_grad, to_odd = call(
        functools.partial(relay_kernel, skip),
        [own_grad, *steps[1], far_out, *far_near_out],
        (sized(steps[1][0].shape[0] - skip + some, BLOCK, BF16),) * 2,
        window,
        scalars=False,
    )
    steps.append(pair_steps(to_odd, far_grad))
    far_first = dp_swap(after(local[:QKV], far_last, far_grad), 2)
    thirds = after(far_last, far_grad)
    far_near_last = [dp_swap(thirds[at : at + HEAD_DIM], 1) for at in range(0, QKV, HEAD_DIM)]
    while len(steps) < count + 1:
        drop = {count - 1: width, count: some}.get(len(steps), 0)
        steps.append(pair_steps(*(ref[drop:] for ref in steps[-1])))

    flat = lambda own, pairs: [own] + [ref for pair in pairs for ref in pair]
    normed_slots = flat(normed, [(first_odd, near_grad)] + steps[1 : count - 1])
    near_slots = flat(near_grad, steps[1:count])
    near_at = [ref.shape[0] - some for ref in near_slots[:3]]
    near_at += [ref.shape[0] - 2 * some for ref in near_slots[3:]]
    far_slots = flat(far_grad, steps[2 : count + 1])
    far_at = [ref.shape[0] - some for ref in far_slots]
    window_normed, total = call(
        functools.partial(first_kernel, count, near_at),
        [doc_ids, *normed_slots, *near_slots, local, *near],
        (sized(width, window, BF16), sized(BLOCK, width, F32)),
        window,
        scratch=[pltpu.VMEM((some, window), BF16)],
    )

    def add(total, places, packs, extra=()):
        return call(
            functools.partial(next_kernel, count, far_at, places, bool(extra)),
            [doc_ids, *far_slots, window_normed, total, *packs, *extra],
            sized(BLOCK, width, BF16 if extra else F32),
            window,
            scratch=[pltpu.VMEM((len(places) * HEAD_DIM, window), BF16)],
        )

    total = add(total, (1, heads + 1), [far_last, *far_near_last])
    far_near_first = dp_swap(after(far_first, total), 1)
    total = add(total, (0,), [far_first])
    result = add(total, (heads,), [far_near_first], [own_input])
    sections = lax.axis_size("section")
    result = lax.ppermute(result, "section", [(i, (i - 1) % sections) for i in range(sections)])
    return result[None, None]


def solution(mesh):
    return jax.shard_map(
        body,
        mesh=mesh,
        in_specs=(
            P("section", "dp", "ctx", None),
            P("section", "dp", "ctx", None),
            P(),
            P("section", None, "dp"),
            P("section", None, "dp"),
            P("section", None, "dp"),
            P("section", "dp", None),
        ),
        out_specs=P("section", "dp", "ctx", None),
        check_vma=False,
    )
```

```python
import functools
import math

import jax
import jax.numpy as jnp
from jax import lax
from jax.experimental import pallas as pl
from jax.experimental.pallas import tpu as pltpu
from jax.sharding import PartitionSpec as P

HEAD_DIM = 80
BLOCK = 128
QKV = 3 * HEAD_DIM
NEAR_CUT = 320
NEG = -1e30
SCALE = HEAD_DIM**-0.5
LOG2E = math.log2(math.e)
F32 = jnp.float32
BF16 = jnp.bfloat16


def dot_nn(a, b):
    return lax.dot_general(a, b, (((1,), (0,)), ((), ())), preferred_element_type=F32)


def dot_nt(a, b):
    return lax.dot_general(a, b, (((1,), (1,)), ((), ())), preferred_element_type=F32)


def split(x):
    high = x.astype(BF16)
    return high, (x - high.astype(F32)).astype(BF16)


def inverse_rms(x):
    return lax.rsqrt(jnp.mean(x * x, axis=-1, keepdims=True) + 1e-05)


def window_flags(ids_ref, count):
    page, me, blocks = lax.axis_index("dp"), lax.axis_index("ctx"), lax.axis_size("ctx")
    mine = ids_ref[page, me]

    def same(at):
        inside = jnp.clip(at, 0, blocks - 1)
        return (inside == at) & (ids_ref[page, inside] == mine)

    flags = []
    for place in range(1, count):
        behind = same(me - place)
        flags.append((behind, behind | same(me + count - place)))
    return flags


def masks(flags):
    ones = jnp.ones((1, BLOCK), F32)
    row_mask = jnp.concatenate([ones] + [ones * valid.astype(F32) for _, valid in flags], axis=1)
    window = row_mask.shape[1]
    first = lax.broadcasted_iota(jnp.int32, (16, window), 0) == 0
    key_bias = jnp.where(first, 1.0 - row_mask, 0.0).astype(BF16)
    query_bias = jnp.where(first, NEG, 0.0).astype(BF16)
    return key_bias, query_bias, row_mask


def heads_backward(packs, grads, normed, key_bias, query_bias, row_mask):
    window = normed.shape[1]
    chunk = min(window, 384)
    qkv = [dot_nn(pack, normed) for pack in packs]
    queries, keys = [], []
    key_rows, value_rows = [], []
    for part in qkv:
        q_high, q_low = split(part[:HEAD_DIM] * (SCALE * LOG2E))
        k_high, k_low = split(part[HEAD_DIM : 2 * HEAD_DIM])
        queries.append(jnp.concatenate([q_high, q_high, q_low, query_bias], axis=0))
        keys.append(jnp.concatenate([k_high, k_low], axis=0))
        key_rows.append(jnp.concatenate([k_high, k_low, k_high, key_bias], axis=0).T)
        value_rows.append(part[2 * HEAD_DIM :].astype(BF16).T)

    heads = range(len(packs))
    own_query, own_key, own_value = [None for _ in heads], [0.0 for _ in heads], [0.0 for _ in heads]
    for start in range(0, window, chunk):
        cols = slice(start, start + chunk)
        scores = [dot_nn(key_rows[h], queries[h][:, cols]) for h in heads]
        dprob = [dot_nn(value_rows[h], grads[h][:, cols]) for h in heads]
        weights, inverse, delta = [], [], []
        for h in heads:
            weights.append(jnp.exp2(scores[h] - jnp.max(scores[h], axis=0, keepdims=True)))
            total = 1.0 / jnp.sum(weights[h], axis=0, keepdims=True)
            delta.append(jnp.sum(weights[h] * dprob[h], axis=0, keepdims=True) * total)
            inverse.append(total * row_mask[:, cols])
        for h in heads:
            prob = weights[h][:BLOCK] * inverse[h]
            dscore = (prob * (dprob[h][:BLOCK] - delta[h])).astype(BF16)
            own_value[h] = own_value[h] + dot_nt(grads[h][:, cols], prob.astype(BF16))
            own_key[h] = own_key[h] + dot_nt(queries[h][HEAD_DIM:QKV, cols], dscore)
            if start == 0:
                dscore_rows = (
                    weights[h][:, :BLOCK]
                    * inverse[h][:, :BLOCK]
                    * (dprob[h][:, :BLOCK] - delta[h][:, :BLOCK])
                ).astype(BF16)
                own_query[h] = dot_nn(keys[h], dscore_rows)
    result = None
    for h in heads:
        q_grad = ((own_query[h][:HEAD_DIM] + own_query[h][HEAD_DIM:]) * SCALE).astype(BF16)
        k_grad = ((own_key[h][:HEAD_DIM] + own_key[h][HEAD_DIM:]) * (1.0 / LOG2E)).astype(BF16)
        rows = jnp.concatenate([q_grad, k_grad, own_value[h].astype(BF16)], axis=0).T
        part = dot_nn(rows, packs[h])
        result = part if result is None else result + part
    return result


def for_place(index, count, flags, fill):
    if index == 0:
        fill(0)
        return
    behind = flags[index - 1][0]
    even = lax.rem(lax.axis_index("ctx"), 2) == 0
    for is_behind, is_even in ((a, b) for a in (True, False) for b in (True, False)):
        distance = index if is_behind else count - index
        slot = 2 * distance - 1 if is_behind != is_even else 2 * distance

        @pl.when((behind == is_behind) & (even == is_even))
        def _():
            fill(slot)


def transposed_normed(input_ref):
    x = input_ref[...].astype(F32)
    return (x * inverse_rms(x)).astype(BF16).T


def pack_kernel(*refs):
    *weights, local_ref, sems = refs
    heads = local_ref.shape[0] // QKV

    def part(ref, at):
        return ref.at[pl.ds(at * HEAD_DIM, HEAD_DIM), :]

    pairs = [(part(weights[at], h), part(local_ref, 3 * h + at)) for h in range(heads) for at in range(3)]
    copies = [pltpu.make_async_copy(*pair, sems.at[i]) for i, pair in enumerate(pairs)]
    for copy in copies:
        copy.start()
    for copy in copies:
        copy.wait()


def start_kernel(input_ref, grad_ref, even_ref, odd_ref, *refs):
    *weight_refs, normed_ref, to_even_ref, to_odd_ref = refs
    width = normed_ref.shape[0]
    normed_ref[...] = transposed_normed(input_ref)
    to_even_ref[:width, :] = transposed_normed(odd_ref)
    to_odd_ref[:width, :] = transposed_normed(even_ref)
    grad_rows(grad_ref, weight_refs, (to_even_ref, to_odd_ref), width)


def grad_rows(grad_ref, weight_refs, rows_refs, start):
    for weight_ref in weight_refs:
        size = weight_ref.shape[0]
        part = dot_nt(weight_ref[...], grad_ref[...]).astype(BF16)
        for rows_ref in rows_refs:
            rows_ref[start : start + size, :] = part
        start += size


def relay_kernel(skip, grad_ref, even_ref, odd_ref, *refs):
    *weight_refs, to_even_ref, to_odd_ref = refs
    rows = even_ref.shape[0] - skip
    to_even_ref[:rows, :] = odd_ref[skip:, :]
    to_odd_ref[:rows, :] = even_ref[skip:, :]
    grad_rows(grad_ref, weight_refs, (to_even_ref, to_odd_ref), rows)


def first_kernel(count, grad_at, ids_ref, *refs):
    slots = 2 * count - 1
    blocks, grad_slots = refs[:slots], refs[slots : 2 * slots]
    *pack_refs, normed_ref, total_ref, window_ref = refs[2 * slots :]
    width, rows = normed_ref.shape[0], window_ref.shape[0]
    flags = window_flags(ids_ref, count)
    for index in range(count):

        def fill(slot):
            cols = pl.ds(index * BLOCK, BLOCK)
            normed_ref[:, cols] = blocks[slot][:width, :]
            window_ref[:, cols] = grad_slots[slot][grad_at[slot] : grad_at[slot] + rows, :]

        for_place(index, count, flags, fill)
    local_ref, *near_refs = pack_refs
    near = jnp.concatenate([ref[...] for ref in near_refs], axis=0)
    starts = range(0, local_ref.shape[0], QKV)
    packs = [local_ref[at : at + QKV, :] for at in starts] + [near[at : at + QKV] for at in starts]
    grads = [window_ref[h * HEAD_DIM : (h + 1) * HEAD_DIM, :] for h in range(len(packs))]
    total_ref[...] = heads_backward(packs, grads, normed_ref[...], *masks(flags))


def next_kernel(count, grad_at, places, last, ids_ref, *refs):
    slots = 2 * count - 1
    grad_slots = refs[:slots]
    normed_ref, so_far_ref, *rest, total_ref, window_ref = refs[slots:]
    if last:
        *rest, input_ref = rest
    flags = window_flags(ids_ref, count)
    for index in range(count):

        def fill(slot):
            cols = pl.ds(index * BLOCK, BLOCK)
            for at, h in enumerate(places):
                to = slice(at * HEAD_DIM, (at + 1) * HEAD_DIM)
                start = grad_at[slot] + h * HEAD_DIM
                window_ref[to, cols] = grad_slots[slot][start : start + HEAD_DIM, :]

        for_place(index, count, flags, fill)
    packs = [rest[0][...]]
    if len(places) > 1:
        packs.append(jnp.concatenate([ref[...] for ref in rest[1:]], axis=0))
    grads = [window_ref[at * HEAD_DIM : (at + 1) * HEAD_DIM, :] for at in range(len(places))]
    total = so_far_ref[...] + heads_backward(packs, grads, normed_ref[...], *masks(flags))
    if last:
        x = input_ref[...].astype(F32)
        inv_rms = inverse_rms(x)
        branch = inv_rms * total - x * inv_rms**3 * jnp.mean(total * x, axis=-1, keepdims=True)
        total_ref[...] = branch.astype(BF16)
    else:
        total_ref[...] = total


def call(kernel, operands, out_shape, window, scratch=(), scalars=True, space=pltpu.VMEM):
    vmem = pl.BlockSpec(memory_space=pltpu.VMEM)
    specs = [pl.BlockSpec(memory_space=pltpu.SMEM)] if scalars else []
    if space != pltpu.VMEM:
        operands = [pltpu.with_memory_space_constraint(ref, space) for ref in operands]
    return pl.pallas_call(
        kernel,
        out_shape=out_shape,
        in_specs=specs + [pl.BlockSpec(memory_space=space)] * (len(operands) - len(specs)),
        out_specs=jax.tree.map(lambda _: vmem, out_shape),
        scratch_shapes=list(scratch),
        compiler_params=pltpu.CompilerParams(vmem_limit_bytes=(8 << 20) + window * (32 << 10)),
        cost_estimate=pl.CostEstimate(flops=1000, bytes_accessed=1000, transcendentals=0),
    )(*operands)


def pair_swap(array, first):
    length, width = lax.axis_size("ctx"), lax.axis_size("dp")
    pairs = []
    for i in range(length):
        low = i - (i - first) % 2
        for d in range(width):
            if low >= 0 and low + 1 < length:
                pairs.append((i * width + d, (2 * low + 1 - i) * width + d))
            else:
                pairs.append((i * width + d, i * width + (d ^ 1)))
    return lax.ppermute(array, ("ctx", "dp"), pairs)


def pair_steps(even, odd):
    return pair_swap(odd, 0), pair_swap(even, 1)


def after(values, *others):
    return lax.optimization_barrier((values, others))[0]


def dp_swap(array, by):
    return lax.ppermute(array, "dp", [(i, i ^ by) for i in range(lax.axis_size("dp"))])


def body(activations, out_grads, doc_ids, query_weight, key_weight, value_weight, out_weight):
    own_input, own_grad = activations[0, 0], out_grads[0, 0]
    width = own_input.shape[-1]
    count = 3 * lax.axis_size("ctx") // 4
    window = count * BLOCK
    heads = query_weight.shape[2] // HEAD_DIM

    sized = lambda rows, columns, dtype: jax.ShapeDtypeStruct((rows, columns), dtype)
    some = 2 * heads * HEAD_DIM

    out_rows = heads * HEAD_DIM
    own_out = out_weight[0]
    far_out = dp_swap(own_out, 2)
    near_out = dp_swap(own_out, 1)
    first = after(own_input, near_out)
    steps = [pair_steps(first, first)]
    local = call(
        pack_kernel,
        [query_weight[0].T, key_weight[0].T, value_weight[0].T],
        sized(heads * QKV, width, BF16),
        window,
        scratch=[pltpu.SemaphoreType.DMA((3 * heads,))],
        scalars=False,
        space=pltpu.HBM,
    )
    ready = after(local, far_out)
    near = [dp_swap(part, 1) for part in (ready[:NEAR_CUT], ready[NEAR_CUT:])]
    far_last = dp_swap(local[QKV : 2 * QKV], 2)

    normed, near_grad, first_odd = call(
        start_kernel,
        [own_input, after(own_grad, far_out), *steps[0], own_out, near_out],
        (sized(width, BLOCK, BF16),) + (sized(width + some, BLOCK, BF16),) * 2,
        window,
        scalars=False,
    )
    steps.append(pair_steps(first_odd, near_grad))
    far_out = after(far_out, normed)
    far_near_out = [dp_swap(far_out[at : at + HEAD_DIM], 1) for at in range(0, out_rows, HEAD_DIM)]
    skip = width if count == 3 else 0
    far_grad, to_odd = call(
        functools.partial(relay_kernel, skip),
        [own_grad, *steps[1], far_out, *far_near_out],
        (sized(steps[1][0].shape[0] - skip + some, BLOCK, BF16),) * 2,
        window,
        scalars=False,
    )
    steps.append(pair_steps(to_odd, far_grad))
    far_first = dp_swap(after(local[:QKV], far_grad), 2)
    thirds = after(far_last, far_grad)
    far_near_last = [dp_swap(thirds[at : at + HEAD_DIM], 1) for at in range(0, QKV, HEAD_DIM)]
    while len(steps) < count + 1:
        drop = {count - 1: width, count: some}.get(len(steps), 0)
        steps.append(pair_steps(*(ref[drop:] for ref in steps[-1])))

    flat = lambda own, pairs: [own] + [ref for pair in pairs for ref in pair]
    normed_slots = flat(normed, [(first_odd, near_grad)] + steps[1 : count - 1])
    near_slots = flat(near_grad, steps[1:count])
    near_at = [ref.shape[0] - some for ref in near_slots[:3]]
    near_at += [ref.shape[0] - 2 * some for ref in near_slots[3:]]
    far_slots = flat(far_grad, steps[2 : count + 1])
    far_at = [ref.shape[0] - some for ref in far_slots]
    window_normed, total = call(
        functools.partial(first_kernel, count, near_at),
        [doc_ids, *normed_slots, *near_slots, local, *near],
        (sized(width, window, BF16), sized(BLOCK, width, F32)),
        window,
        scratch=[pltpu.VMEM((some, window), BF16)],
    )

    def add(total, places, packs, extra=()):
        return call(
            functools.partial(next_kernel, count, far_at, places, bool(extra)),
            [doc_ids, *far_slots, window_normed, total, *packs, *extra],
            sized(BLOCK, width, BF16 if extra else F32),
            window,
            scratch=[pltpu.VMEM((len(places) * HEAD_DIM, window), BF16)],
        )

    total = add(total, (1, heads + 1), [far_last, *far_near_last])
    far_near_first = dp_swap(after(far_first, total), 1)
    total = add(total, (0,), [far_first])
    result = add(total, (heads,), [far_near_first], [own_input])
    sections = lax.axis_size("section")
    result = lax.ppermute(result, "section", [(i, (i - 1) % sections) for i in range(sections)])
    return result[None, None]


def solution(mesh):
    return jax.shard_map(
        body,
        mesh=mesh,
        in_specs=(
            P("section", "dp", "ctx", None),
            P("section", "dp", "ctx", None),
            P(),
            P("section", None, "dp"),
            P("section", None, "dp"),
            P("section", None, "dp"),
            P("section", "dp", None),
        ),
        out_specs=P("section", "dp", "ctx", None),
        check_vma=False,
    )
```

```python
import functools
import math

import jax
import jax.numpy as jnp
from jax import lax
from jax.experimental import pallas as pl
from jax.experimental.pallas import tpu as pltpu
from jax.sharding import PartitionSpec as P

HEAD_DIM = 80
BLOCK = 128
QKV = 3 * HEAD_DIM
NEAR_CUT = 320
NEG = -1e30
SCALE = HEAD_DIM**-0.5
LOG2E = math.log2(math.e)
F32 = jnp.float32
BF16 = jnp.bfloat16


def dot_nn(a, b):
    return lax.dot_general(a, b, (((1,), (0,)), ((), ())), preferred_element_type=F32)


def dot_nt(a, b):
    return lax.dot_general(a, b, (((1,), (1,)), ((), ())), preferred_element_type=F32)


def split(x):
    high = x.astype(BF16)
    return high, (x - high.astype(F32)).astype(BF16)


def inverse_rms(x):
    return lax.rsqrt(jnp.mean(x * x, axis=-1, keepdims=True) + 1e-05)


def window_flags(ids_ref, count):
    page, me, blocks = lax.axis_index("dp"), lax.axis_index("ctx"), lax.axis_size("ctx")
    mine = ids_ref[page, me]

    def same(at):
        inside = jnp.clip(at, 0, blocks - 1)
        return (inside == at) & (ids_ref[page, inside] == mine)

    flags = []
    for place in range(1, count):
        behind = same(me - place)
        flags.append((behind, behind | same(me + count - place)))
    return flags


def masks(flags):
    ones = jnp.ones((1, BLOCK), F32)
    row_mask = jnp.concatenate([ones] + [ones * valid.astype(F32) for _, valid in flags], axis=1)
    window = row_mask.shape[1]
    first = lax.broadcasted_iota(jnp.int32, (16, window), 0) == 0
    key_bias = jnp.where(first, 1.0 - row_mask, 0.0).astype(BF16)
    query_bias = jnp.where(first, NEG, 0.0).astype(BF16)
    return key_bias, query_bias, row_mask


def heads_backward(packs, grads, normed, key_bias, query_bias, row_mask):
    window = normed.shape[1]
    chunk = min(window, 384)
    qkv = [dot_nn(pack, normed) for pack in packs]
    queries, keys = [], []
    key_rows, value_rows = [], []
    for part in qkv:
        q_high, q_low = split(part[:HEAD_DIM] * (SCALE * LOG2E))
        k_high, k_low = split(part[HEAD_DIM : 2 * HEAD_DIM])
        queries.append(jnp.concatenate([q_high, q_high, q_low, query_bias], axis=0))
        keys.append(jnp.concatenate([k_high, k_low], axis=0))
        key_rows.append(jnp.concatenate([k_high, k_low, k_high, key_bias], axis=0).T)
        value_rows.append(part[2 * HEAD_DIM :].astype(BF16).T)

    heads = range(len(packs))
    own_query, own_key, own_value = [None for _ in heads], [0.0 for _ in heads], [0.0 for _ in heads]
    for start in range(0, window, chunk):
        cols = slice(start, start + chunk)
        scores = [dot_nn(key_rows[h], queries[h][:, cols]) for h in heads]
        dprob = [dot_nn(value_rows[h], grads[h][:, cols]) for h in heads]
        weights, inverse, delta = [], [], []
        for h in heads:
            weights.append(jnp.exp2(scores[h] - jnp.max(scores[h], axis=0, keepdims=True)))
            total = 1.0 / jnp.sum(weights[h], axis=0, keepdims=True)
            delta.append(jnp.sum(weights[h] * dprob[h], axis=0, keepdims=True) * total)
            inverse.append(total * row_mask[:, cols])
        for h in heads:
            prob = weights[h][:BLOCK] * inverse[h]
            dscore = (prob * (dprob[h][:BLOCK] - delta[h])).astype(BF16)
            own_value[h] = own_value[h] + dot_nt(grads[h][:, cols], prob.astype(BF16))
            own_key[h] = own_key[h] + dot_nt(queries[h][HEAD_DIM:QKV, cols], dscore)
            if start == 0:
                dscore_rows = (
                    weights[h][:, :BLOCK]
                    * inverse[h][:, :BLOCK]
                    * (dprob[h][:, :BLOCK] - delta[h][:, :BLOCK])
                ).astype(BF16)
                own_query[h] = dot_nn(keys[h], dscore_rows)
    result = None
    for h in heads:
        q_grad = ((own_query[h][:HEAD_DIM] + own_query[h][HEAD_DIM:]) * SCALE).astype(BF16)
        k_grad = ((own_key[h][:HEAD_DIM] + own_key[h][HEAD_DIM:]) * (1.0 / LOG2E)).astype(BF16)
        rows = jnp.concatenate([q_grad, k_grad, own_value[h].astype(BF16)], axis=0).T
        part = dot_nn(rows, packs[h])
        result = part if result is None else result + part
    return result


def for_place(index, count, flags, fill):
    if index == 0:
        fill(0)
        return
    behind = flags[index - 1][0]
    even = lax.rem(lax.axis_index("ctx"), 2) == 0
    for is_behind, is_even in ((a, b) for a in (True, False) for b in (True, False)):
        distance = index if is_behind else count - index
        slot = 2 * distance - 1 if is_behind != is_even else 2 * distance

        @pl.when((behind == is_behind) & (even == is_even))
        def _():
            fill(slot)


def transposed_normed(input_ref):
    x = input_ref[...].astype(F32)
    return (x * inverse_rms(x)).astype(BF16).T


def pack_kernel(*refs):
    *weights, local_ref, sems = refs
    heads = local_ref.shape[0] // QKV

    def part(ref, at):
        return ref.at[pl.ds(at * HEAD_DIM, HEAD_DIM), :]

    pairs = [(part(weights[at], h), part(local_ref, 3 * h + at)) for h in range(heads) for at in range(3)]
    copies = [pltpu.make_async_copy(*pair, sems.at[i]) for i, pair in enumerate(pairs)]
    for copy in copies:
        copy.start()
    for copy in copies:
        copy.wait()


def start_kernel(input_ref, grad_ref, even_ref, odd_ref, *refs):
    *weight_refs, normed_ref, to_even_ref, to_odd_ref = refs
    width = normed_ref.shape[0]
    normed_ref[...] = transposed_normed(input_ref)
    to_even_ref[:width, :] = transposed_normed(odd_ref)
    to_odd_ref[:width, :] = transposed_normed(even_ref)
    grad_rows(grad_ref, weight_refs, (to_even_ref, to_odd_ref), width)


def grad_rows(grad_ref, weight_refs, rows_refs, start):
    for weight_ref in weight_refs:
        size = weight_ref.shape[0]
        part = dot_nt(weight_ref[...], grad_ref[...]).astype(BF16)
        for rows_ref in rows_refs:
            rows_ref[start : start + size, :] = part
        start += size


def relay_kernel(skip, grad_ref, even_ref, odd_ref, *refs):
    *weight_refs, to_even_ref, to_odd_ref = refs
    rows = even_ref.shape[0] - skip
    to_even_ref[:rows, :] = odd_ref[skip:, :]
    to_odd_ref[:rows, :] = even_ref[skip:, :]
    grad_rows(grad_ref, weight_refs, (to_even_ref, to_odd_ref), rows)


def first_kernel(count, grad_at, ids_ref, *refs):
    slots = 2 * count - 1
    blocks, grad_slots = refs[:slots], refs[slots : 2 * slots]
    *pack_refs, normed_ref, total_ref, window_ref = refs[2 * slots :]
    width, rows = normed_ref.shape[0], window_ref.shape[0]
    flags = window_flags(ids_ref, count)
    for index in range(count):

        def fill(slot):
            cols = pl.ds(index * BLOCK, BLOCK)
            normed_ref[:, cols] = blocks[slot][:width, :]
            window_ref[:, cols] = grad_slots[slot][grad_at[slot] : grad_at[slot] + rows, :]

        for_place(index, count, flags, fill)
    local_ref, *near_refs = pack_refs
    near = jnp.concatenate([ref[...] for ref in near_refs], axis=0)
    starts = range(0, local_ref.shape[0], QKV)
    packs = [local_ref[at : at + QKV, :] for at in starts] + [near[at : at + QKV] for at in starts]
    grads = [window_ref[h * HEAD_DIM : (h + 1) * HEAD_DIM, :] for h in range(len(packs))]
    total_ref[...] = heads_backward(packs, grads, normed_ref[...], *masks(flags))


def next_kernel(count, grad_at, places, last, ids_ref, *refs):
    slots = 2 * count - 1
    grad_slots = refs[:slots]
    normed_ref, so_far_ref, *rest, total_ref, window_ref = refs[slots:]
    if last:
        *rest, input_ref = rest
    flags = window_flags(ids_ref, count)
    for index in range(count):

        def fill(slot):
            cols = pl.ds(index * BLOCK, BLOCK)
            for at, h in enumerate(places):
                to = slice(at * HEAD_DIM, (at + 1) * HEAD_DIM)
                start = grad_at[slot] + h * HEAD_DIM
                window_ref[to, cols] = grad_slots[slot][start : start + HEAD_DIM, :]

        for_place(index, count, flags, fill)
    packs = [rest[0][...]]
    if len(places) > 1:
        packs.append(jnp.concatenate([ref[...] for ref in rest[1:]], axis=0))
    grads = [window_ref[at * HEAD_DIM : (at + 1) * HEAD_DIM, :] for at in range(len(places))]
    total = so_far_ref[...] + heads_backward(packs, grads, normed_ref[...], *masks(flags))
    if last:
        x = input_ref[...].astype(F32)
        inv_rms = inverse_rms(x)
        branch = inv_rms * total - x * inv_rms**3 * jnp.mean(total * x, axis=-1, keepdims=True)
        total_ref[...] = branch.astype(BF16)
    else:
        total_ref[...] = total


def call(kernel, operands, out_shape, window, scratch=(), scalars=True, space=pltpu.VMEM):
    vmem = pl.BlockSpec(memory_space=pltpu.VMEM)
    specs = [pl.BlockSpec(memory_space=pltpu.SMEM)] if scalars else []
    if space != pltpu.VMEM:
        operands = [pltpu.with_memory_space_constraint(ref, space) for ref in operands]
    return pl.pallas_call(
        kernel,
        out_shape=out_shape,
        in_specs=specs + [pl.BlockSpec(memory_space=space)] * (len(operands) - len(specs)),
        out_specs=jax.tree.map(lambda _: vmem, out_shape),
        scratch_shapes=list(scratch),
        compiler_params=pltpu.CompilerParams(vmem_limit_bytes=(8 << 20) + window * (32 << 10)),
        cost_estimate=pl.CostEstimate(flops=1000, bytes_accessed=1000, transcendentals=0),
    )(*operands)


def pair_swap(array, first):
    length, width = lax.axis_size("ctx"), lax.axis_size("dp")
    pairs = []
    for i in range(length):
        low = i - (i - first) % 2
        for d in range(width):
            if low >= 0 and low + 1 < length:
                pairs.append((i * width + d, (2 * low + 1 - i) * width + d))
            else:
                pairs.append((i * width + d, i * width + (d ^ 1)))
    return lax.ppermute(array, ("ctx", "dp"), pairs)


def pair_steps(even, odd):
    return pair_swap(odd, 0), pair_swap(even, 1)


def after(values, *others):
    return lax.optimization_barrier((values, others))[0]


def dp_swap(array, by):
    return lax.ppermute(array, "dp", [(i, i ^ by) for i in range(lax.axis_size("dp"))])


def body(activations, out_grads, doc_ids, query_weight, key_weight, value_weight, out_weight):
    own_input, own_grad = activations[0, 0], out_grads[0, 0]
    width = own_input.shape[-1]
    count = 3 * lax.axis_size("ctx") // 4
    window = count * BLOCK
    heads = query_weight.shape[2] // HEAD_DIM

    sized = lambda rows, columns, dtype: jax.ShapeDtypeStruct((rows, columns), dtype)
    some = 2 * heads * HEAD_DIM

    out_rows = heads * HEAD_DIM
    own_out = out_weight[0]
    far_out = dp_swap(own_out, 2)
    near_out = dp_swap(own_out, 1)
    first = after(own_input, near_out)
    steps = [pair_steps(first, first)]
    local = call(
        pack_kernel,
        [query_weight[0].T, key_weight[0].T, value_weight[0].T],
        sized(heads * QKV, width, BF16),
        window,
        scratch=[pltpu.SemaphoreType.DMA((3 * heads,))],
        scalars=False,
        space=pltpu.HBM,
    )
    ready = after(local, far_out)
    near = [dp_swap(part, 1) for part in (ready[:NEAR_CUT], ready[NEAR_CUT:])]
    far_last = dp_swap(local[QKV : 2 * QKV], 2)

    normed, near_grad, first_odd = call(
        start_kernel,
        [own_input, after(own_grad, far_out), *steps[0], own_out, near_out],
        (sized(width, BLOCK, BF16),) + (sized(width + some, BLOCK, BF16),) * 2,
        window,
        scalars=False,
    )
    steps.append(pair_steps(first_odd, near_grad))
    far_out = after(far_out, normed)
    far_near_out = [dp_swap(far_out[at : at + HEAD_DIM], 1) for at in range(0, out_rows, HEAD_DIM)]
    skip = width if count == 3 else 0
    far_grad, to_odd = call(
        functools.partial(relay_kernel, skip),
        [after(own_grad, near[1]), *steps[1], far_out, *far_near_out],
        (sized(steps[1][0].shape[0] - skip + some, BLOCK, BF16),) * 2,
        window,
        scalars=False,
    )
    steps.append(pair_steps(to_odd, far_grad))
    far_first = dp_swap(after(local[:QKV], normed), 2)
    thirds = after(far_last, far_grad)
    far_near_last = [dp_swap(thirds[at : at + HEAD_DIM], 1) for at in range(0, QKV, HEAD_DIM)]
    while len(steps) < count + 1:
        drop = {count - 1: width, count: some}.get(len(steps), 0)
        steps.append(pair_steps(*(ref[drop:] for ref in steps[-1])))

    flat = lambda own, pairs: [own] + [ref for pair in pairs for ref in pair]
    normed_slots = flat(normed, [(first_odd, near_grad)] + steps[1 : count - 1])
    near_slots = flat(near_grad, steps[1:count])
    near_at = [ref.shape[0] - some for ref in near_slots[:3]]
    near_at += [ref.shape[0] - 2 * some for ref in near_slots[3:]]
    far_slots = flat(far_grad, steps[2 : count + 1])
    far_at = [ref.shape[0] - some for ref in far_slots]
    window_normed, total = call(
        functools.partial(first_kernel, count, near_at),
        [doc_ids, *normed_slots, *near_slots, local, *near],
        (sized(width, window, BF16), sized(BLOCK, width, F32)),
        window,
        scratch=[pltpu.VMEM((some, window), BF16)],
    )

    def add(total, places, packs, extra=()):
        return call(
            functools.partial(next_kernel, count, far_at, places, bool(extra)),
            [doc_ids, *far_slots, window_normed, total, *packs, *extra],
            sized(BLOCK, width, BF16 if extra else F32),
            window,
            scratch=[pltpu.VMEM((len(places) * HEAD_DIM, window), BF16)],
        )

    total = add(total, (1, heads + 1), [far_last, *far_near_last])
    far_near_first = dp_swap(after(far_first, total), 1)
    total = add(total, (0,), [far_first])
    result = add(total, (heads,), [far_near_first], [own_input])
    sections = lax.axis_size("section")
    result = lax.ppermute(result, "section", [(i, (i - 1) % sections) for i in range(sections)])
    return result[None, None]


def solution(mesh):
    return jax.shard_map(
        body,
        mesh=mesh,
        in_specs=(
            P("section", "dp", "ctx", None),
            P("section", "dp", "ctx", None),
            P(),
            P("section", None, "dp"),
            P("section", None, "dp"),
            P("section", None, "dp"),
            P("section", "dp", None),
        ),
        out_specs=P("section", "dp", "ctx", None),
        check_vma=False,
    )
```

```python
import functools
import math

import jax
import jax.numpy as jnp
from jax import lax
from jax.experimental import pallas as pl
from jax.experimental.pallas import tpu as pltpu
from jax.sharding import PartitionSpec as P

HEAD_DIM = 80
BLOCK = 128
QKV = 3 * HEAD_DIM
NEAR_CUT = 320
NEG = -1e30
SCALE = HEAD_DIM**-0.5
LOG2E = math.log2(math.e)
F32 = jnp.float32
BF16 = jnp.bfloat16


def dot_nn(a, b):
    return lax.dot_general(a, b, (((1,), (0,)), ((), ())), preferred_element_type=F32)


def dot_nt(a, b):
    return lax.dot_general(a, b, (((1,), (1,)), ((), ())), preferred_element_type=F32)


def split(x):
    high = x.astype(BF16)
    return high, (x - high.astype(F32)).astype(BF16)


def inverse_rms(x):
    return lax.rsqrt(jnp.mean(x * x, axis=-1, keepdims=True) + 1e-05)


def window_flags(ids_ref, count):
    page, me, blocks = lax.axis_index("dp"), lax.axis_index("ctx"), lax.axis_size("ctx")
    mine = ids_ref[page, me]

    def same(at):
        inside = jnp.clip(at, 0, blocks - 1)
        return (inside == at) & (ids_ref[page, inside] == mine)

    flags = []
    for place in range(1, count):
        behind = same(me - place)
        flags.append((behind, behind | same(me + count - place)))
    return flags


def masks(flags):
    ones = jnp.ones((1, BLOCK), F32)
    row_mask = jnp.concatenate([ones] + [ones * valid.astype(F32) for _, valid in flags], axis=1)
    window = row_mask.shape[1]
    first = lax.broadcasted_iota(jnp.int32, (16, window), 0) == 0
    key_bias = jnp.where(first, 1.0 - row_mask, 0.0).astype(BF16)
    query_bias = jnp.where(first, NEG, 0.0).astype(BF16)
    return key_bias, query_bias, row_mask


def heads_backward(packs, grads, normed, key_bias, query_bias, row_mask):
    window = normed.shape[1]
    chunk = min(window, 384)
    qkv = [dot_nn(pack, normed) for pack in packs]
    queries, keys = [], []
    key_rows, value_rows = [], []
    for part in qkv:
        q_high, q_low = split(part[:HEAD_DIM] * (SCALE * LOG2E))
        k_high, k_low = split(part[HEAD_DIM : 2 * HEAD_DIM])
        queries.append(jnp.concatenate([q_high, q_high, q_low, query_bias], axis=0))
        keys.append(jnp.concatenate([k_high, k_low], axis=0))
        key_rows.append(jnp.concatenate([k_high, k_low, k_high, key_bias], axis=0).T)
        value_rows.append(part[2 * HEAD_DIM :].astype(BF16).T)

    heads = range(len(packs))
    own_query, own_key, own_value = [None for _ in heads], [0.0 for _ in heads], [0.0 for _ in heads]
    for start in range(0, window, chunk):
        cols = slice(start, start + chunk)
        scores = [dot_nn(key_rows[h], queries[h][:, cols]) for h in heads]
        dprob = [dot_nn(value_rows[h], grads[h][:, cols]) for h in heads]
        weights, inverse, delta = [], [], []
        for h in heads:
            weights.append(jnp.exp2(scores[h] - jnp.max(scores[h], axis=0, keepdims=True)))
            total = 1.0 / jnp.sum(weights[h], axis=0, keepdims=True)
            delta.append(jnp.sum(weights[h] * dprob[h], axis=0, keepdims=True) * total)
            inverse.append(total * row_mask[:, cols])
        for h in heads:
            prob = weights[h][:BLOCK] * inverse[h]
            dscore = (prob * (dprob[h][:BLOCK] - delta[h])).astype(BF16)
            own_value[h] = own_value[h] + dot_nt(grads[h][:, cols], prob.astype(BF16))
            own_key[h] = own_key[h] + dot_nt(queries[h][HEAD_DIM:QKV, cols], dscore)
            if start == 0:
                dscore_rows = (
                    weights[h][:, :BLOCK]
                    * inverse[h][:, :BLOCK]
                    * (dprob[h][:, :BLOCK] - delta[h][:, :BLOCK])
                ).astype(BF16)
                own_query[h] = dot_nn(keys[h], dscore_rows)
    result = None
    for h in heads:
        q_grad = ((own_query[h][:HEAD_DIM] + own_query[h][HEAD_DIM:]) * SCALE).astype(BF16)
        k_grad = ((own_key[h][:HEAD_DIM] + own_key[h][HEAD_DIM:]) * (1.0 / LOG2E)).astype(BF16)
        rows = jnp.concatenate([q_grad, k_grad, own_value[h].astype(BF16)], axis=0).T
        part = dot_nn(rows, packs[h])
        result = part if result is None else result + part
    return result


def for_place(index, count, flags, fill):
    if index == 0:
        fill(0)
        return
    behind = flags[index - 1][0]
    even = lax.rem(lax.axis_index("ctx"), 2) == 0
    for is_behind, is_even in ((a, b) for a in (True, False) for b in (True, False)):
        distance = index if is_behind else count - index
        slot = 2 * distance - 1 if is_behind != is_even else 2 * distance

        @pl.when((behind == is_behind) & (even == is_even))
        def _():
            fill(slot)


def transposed_normed(input_ref):
    x = input_ref[...].astype(F32)
    return (x * inverse_rms(x)).astype(BF16).T


def pack_kernel(*refs):
    *weights, local_ref, sems = refs
    heads = local_ref.shape[0] // QKV

    def part(ref, at):
        return ref.at[pl.ds(at * HEAD_DIM, HEAD_DIM), :]

    pairs = [(part(weights[at], h), part(local_ref, 3 * h + at)) for h in range(heads) for at in range(3)]
    copies = [pltpu.make_async_copy(*pair, sems.at[i]) for i, pair in enumerate(pairs)]
    for copy in copies:
        copy.start()
    for copy in copies:
        copy.wait()


def start_kernel(input_ref, grad_ref, even_ref, odd_ref, *refs):
    *weight_refs, normed_ref, to_even_ref, to_odd_ref = refs
    width = normed_ref.shape[0]
    normed_ref[...] = transposed_normed(input_ref)
    to_even_ref[:width, :] = transposed_normed(odd_ref)
    to_odd_ref[:width, :] = transposed_normed(even_ref)
    grad_rows(grad_ref, weight_refs, (to_even_ref, to_odd_ref), width)


def grad_rows(grad_ref, weight_refs, rows_refs, start):
    for weight_ref in weight_refs:
        size = weight_ref.shape[0]
        part = dot_nt(weight_ref[...], grad_ref[...]).astype(BF16)
        for rows_ref in rows_refs:
            rows_ref[start : start + size, :] = part
        start += size


def relay_kernel(skip, grad_ref, even_ref, odd_ref, *refs):
    *weight_refs, to_even_ref, to_odd_ref = refs
    rows = even_ref.shape[0] - skip
    to_even_ref[:rows, :] = odd_ref[skip:, :]
    to_odd_ref[:rows, :] = even_ref[skip:, :]
    grad_rows(grad_ref, weight_refs, (to_even_ref, to_odd_ref), rows)


def first_kernel(count, grad_at, ids_ref, *refs):
    slots = 2 * count - 1
    blocks, grad_slots = refs[:slots], refs[slots : 2 * slots]
    *pack_refs, normed_ref, total_ref, window_ref = refs[2 * slots :]
    width, rows = normed_ref.shape[0], window_ref.shape[0]
    flags = window_flags(ids_ref, count)
    for index in range(count):

        def fill(slot):
            cols = pl.ds(index * BLOCK, BLOCK)
            normed_ref[:, cols] = blocks[slot][:width, :]
            window_ref[:, cols] = grad_slots[slot][grad_at[slot] : grad_at[slot] + rows, :]

        for_place(index, count, flags, fill)
    local_ref, *near_refs = pack_refs
    near = jnp.concatenate([ref[...] for ref in near_refs], axis=0)
    starts = range(0, local_ref.shape[0], QKV)
    packs = [local_ref[at : at + QKV, :] for at in starts] + [near[at : at + QKV] for at in starts]
    grads = [window_ref[h * HEAD_DIM : (h + 1) * HEAD_DIM, :] for h in range(len(packs))]
    total_ref[...] = heads_backward(packs, grads, normed_ref[...], *masks(flags))


def next_kernel(count, grad_at, places, last, ids_ref, *refs):
    slots = 2 * count - 1
    grad_slots = refs[:slots]
    normed_ref, so_far_ref, *rest, total_ref, window_ref = refs[slots:]
    if last:
        *rest, input_ref = rest
    flags = window_flags(ids_ref, count)
    for index in range(count):

        def fill(slot):
            cols = pl.ds(index * BLOCK, BLOCK)
            for at, h in enumerate(places):
                to = slice(at * HEAD_DIM, (at + 1) * HEAD_DIM)
                start = grad_at[slot] + h * HEAD_DIM
                window_ref[to, cols] = grad_slots[slot][start : start + HEAD_DIM, :]

        for_place(index, count, flags, fill)
    packs = [rest[0][...]]
    if len(places) > 1:
        packs.append(jnp.concatenate([ref[...] for ref in rest[1:]], axis=0))
    grads = [window_ref[at * HEAD_DIM : (at + 1) * HEAD_DIM, :] for at in range(len(places))]
    total = so_far_ref[...] + heads_backward(packs, grads, normed_ref[...], *masks(flags))
    if last:
        x = input_ref[...].astype(F32)
        inv_rms = inverse_rms(x)
        branch = inv_rms * total - x * inv_rms**3 * jnp.mean(total * x, axis=-1, keepdims=True)
        total_ref[...] = branch.astype(BF16)
    else:
        total_ref[...] = total


def call(kernel, operands, out_shape, window, scratch=(), scalars=True, space=pltpu.VMEM):
    vmem = pl.BlockSpec(memory_space=pltpu.VMEM)
    specs = [pl.BlockSpec(memory_space=pltpu.SMEM)] if scalars else []
    if space != pltpu.VMEM:
        operands = [pltpu.with_memory_space_constraint(ref, space) for ref in operands]
    return pl.pallas_call(
        kernel,
        out_shape=out_shape,
        in_specs=specs + [pl.BlockSpec(memory_space=space)] * (len(operands) - len(specs)),
        out_specs=jax.tree.map(lambda _: vmem, out_shape),
        scratch_shapes=list(scratch),
        compiler_params=pltpu.CompilerParams(vmem_limit_bytes=(8 << 20) + window * (32 << 10)),
        cost_estimate=pl.CostEstimate(flops=1000, bytes_accessed=1000, transcendentals=0),
    )(*operands)


def pair_swap(array, first):
    length, width = lax.axis_size("ctx"), lax.axis_size("dp")
    pairs = []
    for i in range(length):
        low = i - (i - first) % 2
        for d in range(width):
            if low >= 0 and low + 1 < length:
                pairs.append((i * width + d, (2 * low + 1 - i) * width + d))
            else:
                pairs.append((i * width + d, i * width + (d ^ 1)))
    return lax.ppermute(array, ("ctx", "dp"), pairs)


def pair_steps(even, odd):
    return pair_swap(odd, 0), pair_swap(even, 1)


def after(values, *others):
    return lax.optimization_barrier((values, others))[0]


def dp_swap(array, by):
    return lax.ppermute(array, "dp", [(i, i ^ by) for i in range(lax.axis_size("dp"))])


def body(activations, out_grads, doc_ids, query_weight, key_weight, value_weight, out_weight):
    own_input, own_grad = activations[0, 0], out_grads[0, 0]
    width = own_input.shape[-1]
    count = 3 * lax.axis_size("ctx") // 4
    window = count * BLOCK
    heads = query_weight.shape[2] // HEAD_DIM

    sized = lambda rows, columns, dtype: jax.ShapeDtypeStruct((rows, columns), dtype)
    some = 2 * heads * HEAD_DIM

    out_rows = heads * HEAD_DIM
    own_out = out_weight[0]
    far_out = dp_swap(own_out, 2)
    near_out = dp_swap(own_out, 1)
    first = after(own_input, near_out)
    steps = [pair_steps(first, first)]
    local = call(
        pack_kernel,
        [query_weight[0].T, key_weight[0].T, value_weight[0].T],
        sized(heads * QKV, width, BF16),
        window,
        scratch=[pltpu.SemaphoreType.DMA((3 * heads,))],
        scalars=False,
        space=pltpu.HBM,
    )
    ready = after(local, far_out)
    near = [dp_swap(part, 1) for part in (ready[:NEAR_CUT], ready[NEAR_CUT:])]
    far_last = dp_swap(local[QKV : 2 * QKV], 2)

    normed, near_grad, first_odd = call(
        start_kernel,
        [own_input, after(own_grad, far_out), *steps[0], own_out, near_out],
        (sized(width, BLOCK, BF16),) + (sized(width + some, BLOCK, BF16),) * 2,
        window,
        scalars=False,
    )
    steps.append(pair_steps(first_odd, near_grad))
    far_out = after(far_out, normed)
    far_near_out = [dp_swap(far_out[at : at + HEAD_DIM], 1) for at in range(0, out_rows, HEAD_DIM)]
    skip = width if count == 3 else 0
    far_grad, to_odd = call(
        functools.partial(relay_kernel, skip),
        [after(own_grad, near[1]), *steps[1], far_out, *far_near_out],
        (sized(steps[1][0].shape[0] - skip + some, BLOCK, BF16),) * 2,
        window,
        scalars=False,
    )
    steps.append(pair_steps(to_odd, far_grad))
    far_first = dp_swap(after(local[:QKV], normed), 2)
    thirds = after(far_last, far_grad)
    far_near_last = [dp_swap(thirds[at : at + HEAD_DIM], 1) for at in range(0, QKV, HEAD_DIM)]
    while len(steps) < count + 1:
        drop = {count - 1: width, count: some}.get(len(steps), 0)
        steps.append(pair_steps(*(ref[drop:] for ref in steps[-1])))

    flat = lambda own, pairs: [own] + [ref for pair in pairs for ref in pair]
    normed_slots = flat(normed, [(first_odd, near_grad)] + steps[1 : count - 1])
    near_slots = flat(near_grad, steps[1:count])
    near_at = [ref.shape[0] - some for ref in near_slots[:3]]
    near_at += [ref.shape[0] - 2 * some for ref in near_slots[3:]]
    far_slots = flat(far_grad, steps[2 : count + 1])
    far_at = [ref.shape[0] - some for ref in far_slots]
    window_normed, total = call(
        functools.partial(first_kernel, count, near_at),
        [doc_ids, *normed_slots, *near_slots, local, *near],
        (sized(width, window, BF16), sized(BLOCK, width, F32)),
        window,
        scratch=[pltpu.VMEM((some, window), BF16)],
    )

    def add(total, places, packs, extra=()):
        return call(
            functools.partial(next_kernel, count, far_at, places, bool(extra)),
            [doc_ids, *far_slots, window_normed, total, *packs, *extra],
            sized(BLOCK, width, BF16 if extra else F32),
            window,
            scratch=[pltpu.VMEM((len(places) * HEAD_DIM, window), BF16)],
        )

    far_near_first = dp_swap(after(far_first, total, steps[-1], far_near_last), 1)
    total = add(total, (1, heads + 1), [far_last, *far_near_last])
    result = add(total, (0, heads), [far_first, far_near_first], [own_input])
    sections = lax.axis_size("section")
    result = lax.ppermute(result, "section", [(i, (i - 1) % sections) for i in range(sections)])
    return result[None, None]


def solution(mesh):
    return jax.shard_map(
        body,
        mesh=mesh,
        in_specs=(
            P("section", "dp", "ctx", None),
            P("section", "dp", "ctx", None),
            P(),
            P("section", None, "dp"),
            P("section", None, "dp"),
            P("section", None, "dp"),
            P("section", "dp", None),
        ),
        out_specs=P("section", "dp", "ctx", None),
        check_vma=False,
    )
```
